512 devices in a mesh: tile: 128 (over z, y, core), filt: 4 (over x).
Axes of the slice: x: 4, y: 8, z: 8, core: 2. Of those that a mesh axis runs over, the one named last changes fastest.
Arguments:
- activations: bfloat16 [128, 2, 8, 8, 256], P('tile', None, None, None, 'filt'), may hold values from -6 to 6
- out_grad: bfloat16 [128, 2, 8, 8, 512], P('tile', None, None, None, 'filt'), may hold values from -6 to 6
- kernel: bfloat16 [3, 3, 3, 256, 512], P(None, None, None, None, 'filt'), may hold values from -0.078125 to 0.078125
Outputs:
- input_grad: bfloat16 [128, 2, 8, 8, 256], P('tile', None, None, None, 'filt')
- weight_grad: bfloat16 [3, 3, 3, 256, 512], P(None, None, None, None, 'filt')
The draws below stay inside these ranges and needn't reach their ends.
All inputs are finite; a program needn't handle non-finite values.
Results may differ from the reference program's by a relative error of at most 0.0015.
Values may be sent and summed in bfloat16 or wider, within the bound.
No kernel may reach another device: no remote copies, remote signals or barrier semaphores. Data moves between devices by JAX's collectives and lax.ppermute only.
A program may use at most 128 MiB of HBM per device.

```python
import math
import jax
import jax.numpy as jnp

CIN = 256
COUT = 512
FRAMES = 2
TH = 8
TW = 8
CLIPS = 2
GX = 8
GY = 8
TILES = 128


def shard_levels(key, dims, split, smallest, high):
    loudness, own = 1.0, jax.random.fold_in(key, 6)
    for dim, parts in split:
        heights = jnp.exp(jax.random.uniform(jax.random.fold_in(own, dim), (parts,), jnp.float32, smallest / len(split), high / len(split)))
        loudness = loudness * jnp.repeat(heights, dims[dim] // parts).reshape([-1 if axis == dim else 1 for axis in range(len(dims))])
    return loudness


def noise(own_key, dims, scale, bound, split=(), dtype=jnp.bfloat16):
    drawn = scale * jax.random.normal(own_key, dims, jnp.float32)
    if split:
        drawn = drawn * shard_levels(own_key, dims, split, -0.22, 0.18)
    return jnp.clip(drawn, -bound, bound).astype(dtype)


def setup_inputs(seed: int = 0) -> dict:
    key_list = jax.random.split(jax.random.key(seed), 4)
    activations = noise(key_list[0], (TILES, FRAMES, TH, TW, CIN), 1.0, 6.0, ((0, 128), (4, 4)))
    out_grad = noise(key_list[1], (TILES, FRAMES, TH, TW, COUT), 1.0, 6.0, ((0, 128), (4, 4)))
    kernel = noise(key_list[2], (3, 3, 3, CIN, COUT), (27 * CIN) ** -0.5, 0.078125, ((4, 4),))
    return {"activations": activations, "out_grad": out_grad, "kernel": kernel}


def to_grid(tiled, channels):
    shaped = tiled.reshape(GY, GX, CLIPS, FRAMES, TH, TW, channels)
    shaped = jnp.transpose(shaped, (2, 3, 0, 4, 1, 5, 6))
    return shaped.reshape(CLIPS, FRAMES, GY * TH, GX * TW, channels)

def from_grid(grid, channels):
    shaped = grid.reshape(CLIPS, FRAMES, GY, TH, GX, TW, channels)
    shaped = jnp.transpose(shaped, (2, 4, 0, 1, 3, 5, 6))
    return shaped.reshape(GY * GX * CLIPS, FRAMES, TH, TW, channels)

def reference(activations, out_grad, kernel):
    height = GY * TH
    width = GX * TW
    count = CLIPS * FRAMES * height * width
    xgrid = jnp.pad(to_grid(activations, CIN), ((0, 0), (1, 1), (1, 1), (1, 1), (0, 0)))
    ggrid = to_grid(out_grad, COUT)
    gpad = jnp.pad(ggrid, ((0, 0), (1, 1), (1, 1), (1, 1), (0, 0)))
    grows = ggrid.reshape(count, COUT)
    total = jnp.zeros((count, CIN), jnp.float32)
    taps = []
    for ta in range(3):
        for tb in range(3):
            for te in range(3):
                gslice = gpad[:, 2 - ta:2 - ta + FRAMES, 2 - tb:2 - tb + height, 2 - te:2 - te + width, :]
                total = total + jnp.dot(gslice.reshape(count, COUT), kernel[ta, tb, te].T, preferred_element_type=jnp.float32)
                xslice = xgrid[:, ta:ta + FRAMES, tb:tb + height, te:te + width, :]
                taps.append(jnp.dot(xslice.reshape(count, CIN).T, grows, preferred_element_type=jnp.float32))
    input_grad = from_grid(total.reshape(CLIPS, FRAMES, height, width, CIN), CIN).astype(jnp.bfloat16)
    scale = 1.0 / math.sqrt(TILES * FRAMES * TH * TW)
    weight_grad = (jnp.stack(taps).reshape(3, 3, 3, CIN, COUT) * scale).astype(jnp.bfloat16)
    return (input_grad, weight_grad)
```

```python
import math

import jax
import jax.numpy as jnp
from jax import lax
from jax.experimental import pallas as pl
from jax.experimental.pallas import tpu as pltpu
from jax.sharding import Mesh
from jax.sharding import PartitionSpec as P

AXES = ("z", "y", "core", "x")
TILE = ("z", "y", "core")
NZ, NY, NC, NX = 8, 8, 2, 4
F, H, W = 2, 8, 8
CIN, COUT = 256, 512
CI, CO = CIN // NX, COUT // NX
GROWS = F * (H + 2) * W
CJ = CI // NY
XROWS = 16
CHUNK = 7 * CJ


def tile_index(z, y, core):
    return (z * NY + y) * NC + core


SPARSE = [
    [tile_index(a + 2 * i, b + 2 * j, c) for i in range(4) for j in range(4)]
    for a in range(2)
    for b in range(2)
    for c in range(NC)
]
BLOCKS = [
    [tile_index(2 * i + a, 2 * j + b, c) for a in range(2) for b in range(2)]
    for i in range(4)
    for j in range(4)
    for c in range(NC)
]


def shifted(own, left, right, tap):
    if tap == 1:
        return own
    row = lax.broadcasted_iota(jnp.int32, own.shape, own.ndim - 2)
    axis = own.ndim - 2
    if tap == 0:
        return jnp.where(row == W - 1, pltpu.roll(right, W - 1, axis), pltpu.roll(own, W - 1, axis))
    return jnp.where(row == 0, pltpu.roll(left, 1, axis), pltpu.roll(own, 1, axis))


def input_kernel(col_ref, g_ref, k_ref, out_ref):
    col = col_ref[0]

    def tile(i):
        return g_ref[i, :GROWS, :].astype(jnp.float32).reshape(F * (H + 2), W, CO)

    own = tile(col)
    left = jnp.where(col > 0, tile(jnp.maximum(col - 1, 0)), 0.0)
    right = jnp.where(col < NY - 1, tile(jnp.minimum(col + 1, NY - 1)), 0.0)
    acc0 = jnp.zeros((H * W, CIN), jnp.float32)
    acc1 = jnp.zeros((H * W, CIN), jnp.float32)
    dims = (((1,), (1,)), ((), ()))
    for te in range(3):
        moved = shifted(own, left, right, te).reshape(F, H + 2, W, CO)
        for tb in range(3):
            rows = moved[:, 2 - tb : 2 - tb + H].reshape(F, H * W, CO).astype(jnp.bfloat16)
            both = jnp.concatenate([rows[0], rows[1]], axis=1)
            k0, k1, k2 = (k_ref[ta * 9 + tb * 3 + te] for ta in range(3))
            acc0 += lax.dot_general(
                both, jnp.concatenate([k1, k0], axis=1), dims, preferred_element_type=jnp.float32
            )
            acc1 += lax.dot_general(
                both, jnp.concatenate([k2, k1], axis=1), dims, preferred_element_type=jnp.float32
            )
    for i in range(NX):
        cut = slice(i * CI, (i + 1) * CI)
        out_ref[i] = jnp.concatenate([acc0[:, cut], acc1[:, cut]], axis=1)


def weight_kernel(g_ref, x_ref, out_ref):
    own = g_ref[:, :GROWS, :].astype(jnp.float32).reshape(NY, F * (H + 2), W, CO)
    edge = jnp.zeros((1, F * (H + 2), W, CO), jnp.float32)
    left = jnp.concatenate([edge, own[:-1]], axis=0)
    right = jnp.concatenate([own[1:], edge], axis=0)
    x = x_ref[...].reshape(NX, NY, CJ, F * H * W)
    frames = []
    for f in range(F):
        cut = slice(f * H * W, (f + 1) * H * W)
        cols = [x[:, y, :, cut].reshape(NX * CJ, H * W) for y in range(NY)]
        frames.append(jnp.concatenate(cols, axis=1))
    xs = jnp.concatenate(frames, axis=0).astype(jnp.bfloat16)
    half = NX * CJ
    for te in range(3):
        moved = shifted(own, left, right, te).reshape(NY, F, H + 2, W, CO)
        for tb in range(3):
            rows = moved[:, :, 2 - tb : 2 - tb + H].astype(jnp.bfloat16)
            g0 = rows[:, 0].reshape(NY * H * W, CO)
            g1 = rows[:, 1].reshape(NY * H * W, CO)
            both = jnp.concatenate([g0, g1], axis=1)
            prod = jnp.dot(xs, both, preferred_element_type=jnp.float32)
            parts = (
                prod[:half, CO:],
                prod[:half, :CO] + prod[half:, CO:],
                prod[half:, :CO],
            )
            for ta in range(3):
                group, t = divmod(ta * 9 + tb * 3 + te, 7)
                for q in range(NX):
                    out_ref[(group // 2) * 8 + q * 2 + group % 2, t * CJ : (t + 1) * CJ, :] = parts[
                        ta
                    ][q * CJ : (q + 1) * CJ]
    for q in range(NX):
        out_ref[8 + q * 2 + 1, 6 * CJ : 7 * CJ, :] = jnp.zeros((CJ, CO), jnp.float32)


def shards(activations, out_grad, kernel):
    col = lax.axis_index("y")
    core = lax.axis_index("core")
    g = out_grad[0]
    with jax.named_scope("halo"):
        north = lax.ppermute(g[:, -1:], "z", [(i, i + 1) for i in range(NZ - 1)])
        south = lax.ppermute(g[:, :1], "z", [(i + 1, i) for i in range(NZ - 1)])
        tall = jnp.concatenate([north, g, south], axis=1).reshape(GROWS, CO)
    with jax.named_scope("strip"):
        xt = activations[0].reshape(F * H * W, CI).T.reshape(NY, CJ, F * H * W)
        xt = jnp.pad(xt, ((0, 0), (0, XROWS - CJ), (0, 0)))
        send = jnp.concatenate([jnp.broadcast_to(tall, (NY, GROWS, CO)), xt], axis=1)
        strip = lax.all_to_all(send, "y", 0, 0, tiled=True)
    with jax.named_scope("input_part"):
        terms = pl.pallas_call(
            input_kernel,
            out_shape=jax.ShapeDtypeStruct((NX, H * W, F * CI), jnp.float32),
            in_specs=[
                pl.BlockSpec(memory_space=pltpu.SMEM),
                pl.BlockSpec(memory_space=pltpu.VMEM),
                pl.BlockSpec(memory_space=pltpu.VMEM),
            ],
            out_specs=pl.BlockSpec(memory_space=pltpu.VMEM),
            compiler_params=pltpu.CompilerParams(vmem_limit_bytes=32 * 1024 * 1024),
        )(col.reshape(1).astype(jnp.int32), strip, kernel.reshape(27, CIN, CO))
    with jax.named_scope("filters"):
        xmine = strip[:, GROWS : GROWS + CJ].reshape(NY * CJ, F * H * W).astype(jnp.float32)
        send = jnp.concatenate([terms, jnp.broadcast_to(xmine, (NX,) + xmine.shape)], axis=1)
        got = lax.all_to_all(send, "x", 0, 0, tiled=True)
    with jax.named_scope("weight_part"):
        local = pl.pallas_call(
            weight_kernel,
            out_shape=jax.ShapeDtypeStruct((NZ * NC, CHUNK, CO), jnp.float32),
            in_specs=[pl.BlockSpec(memory_space=pltpu.VMEM)] * 2,
            out_specs=pl.BlockSpec(memory_space=pltpu.VMEM),
            compiler_params=pltpu.CompilerParams(vmem_limit_bytes=32 * 1024 * 1024),
        )(strip, got[:, H * W :])
    with jax.named_scope("weight_sum"):
        shares = lax.all_to_all(local, ("z", "core"), 0, 0, tiled=True)
        scale = 1.0 / math.sqrt(NZ * NY * NC * F * H * W)
        mine = (jnp.sum(shares, axis=0) * scale).astype(jnp.bfloat16)
    with jax.named_scope("gather_far"):
        far = lax.all_to_all(
            jnp.broadcast_to(mine, (16, CHUNK, CO)), TILE, 0, 0, axis_index_groups=SPARSE, tiled=True
        )
    with jax.named_scope("gather_near"):
        near = lax.all_to_all(
            jnp.broadcast_to(far, (4, 16, CHUNK, CO)), TILE, 0, 0, axis_index_groups=BLOCKS, tiled=True
        )
    with jax.named_scope("order"):
        near = near.reshape(2, 2, 2, 2, 4, 7, CJ, CO)
        half = jnp.transpose(near, (2, 5, 3, 0, 4, 1, 6, 7)).reshape(2, 7, CIN, CO)
    with jax.named_scope("swap"):
        other = lax.ppermute(half, "core", [(0, 1), (1, 0)])
        first = jnp.where(core == 0, half, other)
        second = jnp.where(core == 0, other, half)
        full = jnp.stack([first, second], axis=1).reshape(28, CIN, CO)
        weight_grad = full[:27].reshape(3, 3, 3, CIN, CO)
    with jax.named_scope("input_sum"):
        total = jnp.sum(got[:, : H * W], axis=0).astype(jnp.bfloat16)
        input_grad = jnp.transpose(total.reshape(H, W, F, CI), (2, 0, 1, 3))[None]
    return (input_grad, weight_grad)


def solution(mesh):
    grid = Mesh(mesh.devices.reshape(NZ, NY, NC, NX), AXES)
    in_specs = (
        P(TILE, None, None, None, "x"),
        P(TILE, None, None, None, "x"),
        P(None, None, None, None, "x"),
    )
    out_specs = (P(TILE, None, None, None, "x"), P(None, None, None, None, "x"))
    return jax.shard_map(shards, mesh=grid, in_specs=in_specs, out_specs=out_specs, check_vma=False)
```

```python
import math

import jax
import jax.numpy as jnp
from jax import lax
from jax.experimental import pallas as pl
from jax.experimental.pallas import tpu as pltpu
from jax.sharding import Mesh
from jax.sharding import PartitionSpec as P

AXES = ("z", "y", "core", "x")
TILE = ("z", "y", "core")
NZ, NY, NC, NX = 8, 8, 2, 4
F, H, W = 2, 8, 8
CIN, COUT = 256, 512
CI, CO = CIN // NX, COUT // NX
GROWS = F * H * W
EXT = (H + 2) * W
CJ = CI // NY
XROWS = 16
TERMS = 2 * EXT
CHUNK = 7 * CJ


def tile_index(z, y, core):
    return (z * NY + y) * NC + core


SPARSE = [
    [tile_index(a + 2 * i, b + 2 * j, c) for i in range(4) for j in range(4)]
    for a in range(2)
    for b in range(2)
    for c in range(NC)
]
BLOCKS = [
    [tile_index((2 * i + pz) % NZ, (2 * j + py) % NY, c) for pz in offsets for py in offsets]
    for i in range(NZ // 2)
    for j in range(NY // 2)
    for c, offsets in enumerate(((0, 1), (2, 1)))
]


def shifted(own, left, right, tap):
    if tap == 1:
        return own
    row = lax.broadcasted_iota(jnp.int32, own.shape, own.ndim - 2)
    axis = own.ndim - 2
    if tap == 0:
        return jnp.where(row == W - 1, pltpu.roll(right, W - 1, axis), pltpu.roll(own, W - 1, axis))
    return jnp.where(row == 0, pltpu.roll(left, 1, axis), pltpu.roll(own, 1, axis))


def input_kernel(col_ref, g_ref, k_ref, out_ref):
    col = col_ref[0]

    def tile(i):
        return g_ref[i, :GROWS, :].astype(jnp.float32).reshape(F * H, W, CO)

    own = tile(col)
    left = jnp.where(col > 0, tile(jnp.maximum(col - 1, 0)), 0.0)
    right = jnp.where(col < NY - 1, tile(jnp.minimum(col + 1, NY - 1)), 0.0)
    dims = (((1,), (1,)), ((), ()))
    sums = [[jnp.zeros((H * W, CIN), jnp.float32) for _ in range(3)] for _ in range(F)]
    for te in range(3):
        rows = shifted(own, left, right, te).reshape(F, H * W, CO).astype(jnp.bfloat16)
        both = jnp.concatenate([rows[0], rows[1]], axis=1)
        for tb in range(3):
            k0, k1, k2 = (k_ref[ta * 9 + tb * 3 + te] for ta in range(3))
            for f, pair in enumerate(((k1, k0), (k2, k1))):
                sums[f][tb] += lax.dot_general(
                    both, jnp.concatenate(pair, axis=1), dims, preferred_element_type=jnp.float32
                )
    tall = []
    for f in range(F):
        total = jnp.zeros((EXT, CIN), jnp.float32)
        for tb in range(3):
            parts = [sums[f][tb]]
            if tb > 0:
                parts.insert(0, jnp.zeros((tb * W, CIN), jnp.float32))
            if tb < 2:
                parts.append(jnp.zeros(((2 - tb) * W, CIN), jnp.float32))
            total += jnp.concatenate(parts, axis=0)
        tall.append(total)
    for i in range(NX):
        cut = slice(i * CI, (i + 1) * CI)
        value = jnp.concatenate([tall[0][:, cut], tall[1][:, cut]], axis=1)
        high = value.astype(jnp.bfloat16)
        out_ref[i, :EXT, :] = high
        out_ref[i, EXT:, :] = (value - high.astype(jnp.float32)).astype(jnp.bfloat16)


def weight_kernel(place_ref, own_ref, pair_ref, north_ref, south_ref, got_ref, out_ref, inner_ref, acc_ref):
    core, row = place_ref[0], place_ref[1]
    terms = got_ref[:, :TERMS, :].astype(jnp.float32)
    terms = terms[:, :EXT, :] + terms[:, EXT:, :]
    terms = (terms[0] + terms[1]) + (terms[2] + terms[3])
    inner_ref[...] = terms[W : EXT - W]
    for z in range(NZ):
        up = jnp.where(row - 1 == z, terms[:W], 0.0)
        out_ref[z, CHUNK:, :] = jnp.where(row + 1 == z, terms[EXT - W :], up)

    x = got_ref[:, TERMS:, :].astype(jnp.float32).reshape(NX, NC, NY, CJ, F * H * W)
    frames = []
    for f in range(F):
        cut = slice(f * H * W, (f + 1) * H * W)
        cols = [
            x[:, clip, y, :, cut].reshape(NX * CJ, H * W) for clip in range(NC) for y in range(NY)
        ]
        frames.append(jnp.concatenate(cols, axis=1))
    xs = jnp.concatenate(frames, axis=0).astype(jnp.bfloat16)
    half = NX * CJ
    talls = []
    for clip, ref in enumerate((own_ref, pair_ref)):
        rows = ref[:, :GROWS, :].astype(jnp.float32).reshape(NY, F, H, W, CO)
        north = north_ref[clip].astype(jnp.float32).reshape(NY, F, 1, W, CO)
        south = south_ref[clip].astype(jnp.float32).reshape(NY, F, 1, W, CO)
        talls.append(jnp.concatenate([north, rows, south], axis=2).reshape(NY, F * (H + 2), W, CO))
    edge = jnp.zeros((1, F * (H + 2), W, CO), jnp.float32)
    for te in range(3):
        moved = []
        for tall in talls:
            left = jnp.concatenate([edge, tall[:-1]], axis=0)
            right = jnp.concatenate([tall[1:], edge], axis=0)
            moved.append(shifted(tall, left, right, te).reshape(NY, F, H + 2, W, CO))
        for tb in range(3):
            cols = []
            for f in range(F):
                rows = [m[:, f, 2 - tb : 2 - tb + H].reshape(NY * H * W, CO) for m in moved]
                cols.append(jnp.concatenate(rows, axis=0).astype(jnp.bfloat16))
            both = jnp.concatenate(cols, axis=1)
            prod = jnp.dot(xs, both, preferred_element_type=jnp.float32)
            parts = (
                prod[:half, CO:],
                prod[:half, :CO] + prod[half:, CO:],
                prod[half:, :CO],
            )
            for ta in range(3):
                group, t = divmod(ta * 9 + tb * 3 + te, 7)
                for q in range(NX):
                    acc_ref[group % 2, (group // 2) * NX + q, t * CJ : (t + 1) * CJ, :] = parts[ta][
                        q * CJ : (q + 1) * CJ
                    ]
    for q in range(NX):
        acc_ref[1, NX + q, 6 * CJ :, :] = jnp.zeros((CJ, CO), jnp.float32)
    out_ref[:, :CHUNK, :] = acc_ref[core]


def shards(activations, out_grad, kernel):
    col = lax.axis_index("y").astype(jnp.int32)
    core = lax.axis_index("core").astype(jnp.int32)
    row = lax.axis_index("z").astype(jnp.int32)
    smem = pl.BlockSpec(memory_space=pltpu.SMEM)
    vmem = pl.BlockSpec(memory_space=pltpu.VMEM)
    params = pltpu.CompilerParams(vmem_limit_bytes=32 * 1024 * 1024)
    swap = [(0, 1), (1, 0)]
    with jax.named_scope("strip"):
        xt = activations[0].reshape(F * H * W, CI).T.reshape(NY, CJ, F * H * W)
        xt = jnp.pad(xt, ((0, 0), (0, XROWS - CJ), (0, 0)))
        rows = jnp.broadcast_to(out_grad[0].reshape(GROWS, CO), (NY, GROWS, CO))
        strip = lax.all_to_all(jnp.concatenate([rows, xt], axis=1), "y", 0, 0, tiled=True)
    with jax.named_scope("clips"):
        pair = lax.ppermute(strip, "core", swap)
    with jax.named_scope("input_part"):
        terms = pl.pallas_call(
            input_kernel,
            out_shape=jax.ShapeDtypeStruct((NX, TERMS, F * CI), jnp.bfloat16),
            in_specs=[smem, vmem, vmem],
            out_specs=vmem,
            compiler_params=params,
        )(col.reshape(1), strip, kernel.reshape(27, CIN, CO))
    with jax.named_scope("edges"):
        both = jnp.stack([strip[:, :GROWS], pair[:, :GROWS]]).reshape(NC, NY, F, H, W, CO)
        north = lax.ppermute(both[:, :, :, H - 1], "z", [(i, i + 1) for i in range(NZ - 1)])
        south = lax.ppermute(both[:, :, :, 0], "z", [(i + 1, i) for i in range(NZ - 1)])
    with jax.named_scope("filters"):
        xmine = [s[:, GROWS : GROWS + CJ].reshape(NY * CJ, F * H * W) for s in (strip, pair)]
        xmine = jnp.broadcast_to(jnp.concatenate(xmine, axis=0), (NX, NC * NY * CJ, F * H * W))
        got = lax.all_to_all(jnp.concatenate([terms, xmine], axis=1), "x", 0, 0, tiled=True)
    with jax.named_scope("weight_part"):
        local, inner = pl.pallas_call(
            weight_kernel,
            out_shape=[
                jax.ShapeDtypeStruct((NZ, CHUNK + W, CO), jnp.float32),
                jax.ShapeDtypeStruct((H * W, F * CI), jnp.float32),
            ],
            in_specs=[smem] + [vmem] * 5,
            out_specs=[vmem] * 2,
            scratch_shapes=[pltpu.VMEM((NC, NZ, CHUNK, CO), jnp.float32)],
            compiler_params=params,
        )(jnp.stack([core, row]), strip, pair, north, south, got)
    with jax.named_scope("weight_sum"):
        shares = lax.all_to_all(local, "z", 0, 0, tiled=True)
        scale = 1.0 / math.sqrt(NZ * NY * NC * F * H * W)
        mine = (jnp.sum(shares[:, :CHUNK], axis=0) * scale).astype(jnp.bfloat16)
    with jax.named_scope("gather_far"):
        far = lax.all_to_all(
            jnp.broadcast_to(mine, (16, CHUNK, CO)), TILE, 0, 0, axis_index_groups=SPARSE, tiled=True
        )
    with jax.named_scope("gather_near"):
        near = lax.all_to_all(
            jnp.broadcast_to(far, (4, 16, CHUNK, CO)), TILE, 0, 0, axis_index_groups=BLOCKS, tiled=True
        )
    with jax.named_scope("order"):
        near = near.reshape(2, 2, 2, 2, 4, 7, CJ, CO)
        half = jnp.transpose(near, (2, 5, 3, 0, 4, 1, 6, 7)).reshape(2, 7, CIN, CO)
    with jax.named_scope("swap"):
        other = lax.ppermute(half, "core", swap)
        first = jnp.where(core == 0, half, other)
        second = jnp.where(core == 0, other, half)
        full = jnp.concatenate([first[0], second[0], first[1], second[1, :6]], axis=0)
        weight_grad = full.reshape(3, 3, 3, CIN, CO)
    with jax.named_scope("input_sum"):
        source = lax.broadcasted_iota(jnp.int32, (NZ, W, F * CI), 0)
        edges = shares[:, CHUNK:]
        above = jnp.sum(jnp.where(source < row, edges, 0.0), axis=0)
        below = jnp.sum(jnp.where(source > row, edges, 0.0), axis=0)
        total = inner.reshape(H, W, F * CI)
        total = jnp.concatenate([total[:1] + above, total[1:-1], total[-1:] + below], axis=0)
        total = total.astype(jnp.bfloat16).reshape(H, W, F, CI)
        input_grad = jnp.transpose(total, (2, 0, 1, 3))[None]
    return (input_grad, weight_grad)


def solution(mesh):
    grid = Mesh(mesh.devices.reshape(NZ, NY, NC, NX), AXES)
    in_specs = (
        P(TILE, None, None, None, "x"),
        P(TILE, None, None, None, "x"),
        P(None, None, None, None, "x"),
    )
    out_specs = (P(TILE, None, None, None, "x"), P(None, None, None, None, "x"))
    return jax.shard_map(shards, mesh=grid, in_specs=in_specs, out_specs=out_specs, check_vma=False)
```

```python
import math

import jax
import jax.numpy as jnp
from jax import lax
from jax.experimental import pallas as pl
from jax.experimental.pallas import tpu as pltpu
from jax.sharding import Mesh
from jax.sharding import PartitionSpec as P

AXES = ("z", "y", "core", "x")
TILE = ("z", "y", "core")
NZ, NY, NC, NX = 8, 8, 2, 4
F, H, W = 2, 8, 8
CIN, COUT = 256, 512
CI, CO = CIN // NX, COUT // NX
GROWS = F * H * W
EXT = (H + 2) * W
CJ = CI // NY
XROWS = 16
TERMS = 2 * EXT
CHUNK = 7 * CJ


def tile_index(z, y, core):
    return (z * NY + y) * NC + core


SPARSE = [
    [tile_index(a + 2 * i, b + 2 * j, c) for i in range(4) for j in range(4)]
    for a in range(2)
    for b in range(2)
    for c in range(NC)
]
BLOCKS = [
    [tile_index((2 * i + pz) % NZ, (2 * j + py) % NY, c) for pz in offsets for py in offsets]
    for i in range(NZ // 2)
    for j in range(NY // 2)
    for c, offsets in enumerate(((0, 1), (2, 1)))
]


def shifted(own, left, right, tap):
    if tap == 1:
        return own
    row = lax.broadcasted_iota(jnp.int32, own.shape, own.ndim - 2)
    axis = own.ndim - 2
    if tap == 0:
        return jnp.where(row == W - 1, pltpu.roll(right, W - 1, axis), pltpu.roll(own, W - 1, axis))
    return jnp.where(row == 0, pltpu.roll(left, 1, axis), pltpu.roll(own, 1, axis))


def input_kernel(col_ref, g_ref, k_ref, out_ref):
    col = col_ref[0]

    def tile(i):
        return g_ref[i, :GROWS, :].astype(jnp.float32).reshape(F * H, W, CO)

    own = tile(col)
    left = jnp.where(col > 0, tile(jnp.maximum(col - 1, 0)), 0.0)
    right = jnp.where(col < NY - 1, tile(jnp.minimum(col + 1, NY - 1)), 0.0)
    dims = (((1,), (1,)), ((), ()))
    sums = [[jnp.zeros((H * W, CIN), jnp.float32) for _ in range(3)] for _ in range(F)]
    for te in range(3):
        rows = shifted(own, left, right, te).reshape(F, H * W, CO).astype(jnp.bfloat16)
        both = jnp.concatenate([rows[0], rows[1]], axis=1)
        for tb in range(3):
            k0, k1, k2 = (k_ref[ta * 9 + tb * 3 + te] for ta in range(3))
            for f, pair in enumerate(((k1, k0), (k2, k1))):
                sums[f][tb] += lax.dot_general(
                    both, jnp.concatenate(pair, axis=1), dims, preferred_element_type=jnp.float32
                )
    tall = []
    for f in range(F):
        total = jnp.zeros((EXT, CIN), jnp.float32)
        for tb in range(3):
            parts = [sums[f][tb]]
            if tb > 0:
                parts.insert(0, jnp.zeros((tb * W, CIN), jnp.float32))
            if tb < 2:
                parts.append(jnp.zeros(((2 - tb) * W, CIN), jnp.float32))
            total += jnp.concatenate(parts, axis=0)
        tall.append(total)
    for i in range(NX):
        cut = slice(i * CI, (i + 1) * CI)
        value = jnp.concatenate([tall[0][:, cut], tall[1][:, cut]], axis=1)
        high = value.astype(jnp.bfloat16)
        out_ref[i, :EXT, :] = high
        out_ref[i, EXT:, :] = (value - high.astype(jnp.float32)).astype(jnp.bfloat16)


def weight_kernel(place_ref, own_ref, pair_ref, edge_ref, got_ref, out_ref, inner_ref, mid_ref):
    core, row = place_ref[0], place_ref[1]
    terms = got_ref[:, :TERMS, :].astype(jnp.float32)
    terms = terms[:, :EXT, :] + terms[:, EXT:, :]
    terms = (terms[0] + terms[1]) + (terms[2] + terms[3])
    inner_ref[...] = terms[W : EXT - W]
    for z in range(NZ):
        up = jnp.where(row - 1 == z, terms[:W], 0.0)
        out_ref[z, CHUNK:, :] = jnp.where(row + 1 == z, terms[EXT - W :], up)

    x = got_ref[:, TERMS:, :].astype(jnp.float32).reshape(NX, NC, NY, CJ, F * H * W)
    frames = []
    for f in range(F):
        cut = slice(f * H * W, (f + 1) * H * W)
        cols = [
            x[:, clip, y, :, cut].reshape(NX * CJ, H * W) for clip in range(NC) for y in range(NY)
        ]
        frames.append(jnp.concatenate(cols, axis=1))
    xs = jnp.concatenate(frames, axis=0).astype(jnp.bfloat16)
    half = NX * CJ
    mids, sides = [], []
    for clip, ref in enumerate((own_ref, pair_ref)):
        rows = ref[:, :GROWS, :].astype(jnp.float32).reshape(NY, F, H, W, CO)
        edge = edge_ref[clip].astype(jnp.float32).reshape(NY, F, 1, W, CO)
        below = jnp.concatenate([rows[:, :, 1:], edge], axis=2)
        above = jnp.concatenate([edge, rows[:, :, :-1]], axis=2)
        mids.append(rows.reshape(NY, F * H, W, CO))
        sides.append(jnp.where(core == 0, below, above).reshape(NY, F * H, W, CO))
    border = jnp.zeros((1, F * H, W, CO), jnp.float32)

    def product(clips, te):
        cols = [[], []]
        for rows in clips:
            left = jnp.concatenate([border, rows[:-1]], axis=0)
            right = jnp.concatenate([rows[1:], border], axis=0)
            moved = shifted(rows, left, right, te).reshape(NY, F, H * W, CO)
            for f in range(F):
                cols[f].append(moved[:, f].reshape(NY * H * W, CO))
        both = [jnp.concatenate(c, axis=0).astype(jnp.bfloat16) for c in cols]
        prod = jnp.dot(xs, jnp.concatenate(both, axis=1), preferred_element_type=jnp.float32)
        return prod[:half, CO:], prod[:half, :CO] + prod[half:, CO:], prod[half:, :CO]

    def put(slot, value):
        group, t = divmod(slot, 7)
        for q in range(NX):
            out_ref[group * NX + q, t * CJ : (t + 1) * CJ, :] = value[q * CJ : (q + 1) * CJ]

    for te in range(3):
        for ta, value in enumerate(product(sides, te)):
            put(ta * 3 + te, value)
        for ta, value in enumerate(product(mids, te)):
            mid_ref[ta * 3 + te] = value
    mid_ref[9] = jnp.zeros((half, CO), jnp.float32)
    for i in range(5):
        put(9 + i, mid_ref[i + 5 * core])


def shards(activations, out_grad, kernel):
    col = lax.axis_index("y").astype(jnp.int32)
    core = lax.axis_index("core").astype(jnp.int32)
    row = lax.axis_index("z").astype(jnp.int32)
    smem = pl.BlockSpec(memory_space=pltpu.SMEM)
    vmem = pl.BlockSpec(memory_space=pltpu.VMEM)
    params = pltpu.CompilerParams(vmem_limit_bytes=32 * 1024 * 1024)
    swap = [(0, 1), (1, 0)]
    with jax.named_scope("strip"):
        xt = activations[0].reshape(F * H * W, CI).T.reshape(NY, CJ, F * H * W)
        xt = jnp.pad(xt, ((0, 0), (0, XROWS - CJ), (0, 0)))
        rows = jnp.broadcast_to(out_grad[0].reshape(GROWS, CO), (NY, GROWS, CO))
        strip = lax.all_to_all(jnp.concatenate([rows, xt], axis=1), "y", 0, 0, tiled=True)
    with jax.named_scope("clips"):
        pair = lax.ppermute(strip, "core", swap)
    with jax.named_scope("input_part"):
        terms = pl.pallas_call(
            input_kernel,
            out_shape=jax.ShapeDtypeStruct((NX, TERMS, F * CI), jnp.bfloat16),
            in_specs=[smem, vmem, vmem],
            out_specs=vmem,
            compiler_params=params,
        )(col.reshape(1), strip, kernel.reshape(27, CIN, CO))
    with jax.named_scope("edges"):
        both = jnp.stack([strip[:, :GROWS], pair[:, :GROWS]]).reshape(NC, NY, F, H, W, CO)
        edge = jnp.where(core == 0, both[:, :, :, 0], both[:, :, :, H - 1])
        route = [(z * NC, (z - 1) * NC) for z in range(1, NZ)]
        route += [(z * NC + 1, (z + 1) * NC + 1) for z in range(NZ - 1)]
        edge = lax.ppermute(edge, ("z", "core"), route)
    with jax.named_scope("filters"):
        xmine = [s[:, GROWS : GROWS + CJ].reshape(NY * CJ, F * H * W) for s in (strip, pair)]
        xmine = jnp.broadcast_to(jnp.concatenate(xmine, axis=0), (NX, NC * NY * CJ, F * H * W))
        got = lax.all_to_all(jnp.concatenate([terms, xmine], axis=1), "x", 0, 0, tiled=True)
    with jax.named_scope("weight_part"):
        local, inner = pl.pallas_call(
            weight_kernel,
            out_shape=[
                jax.ShapeDtypeStruct((NZ, CHUNK + W, CO), jnp.float32),
                jax.ShapeDtypeStruct((H * W, F * CI), jnp.float32),
            ],
            in_specs=[smem] + [vmem] * 4,
            out_specs=[vmem] * 2,
            scratch_shapes=[pltpu.VMEM((10, NX * CJ, CO), jnp.float32)],
            compiler_params=params,
        )(jnp.stack([core, row]), strip, pair, edge, got)
    with jax.named_scope("weight_sum"):
        shares = lax.all_to_all(local, "z", 0, 0, tiled=True)
        scale = 1.0 / math.sqrt(NZ * NY * NC * F * H * W)
        mine = (jnp.sum(shares[:, :CHUNK], axis=0) * scale).astype(jnp.bfloat16)
    with jax.named_scope("gather_far"):
        far = lax.all_to_all(
            jnp.broadcast_to(mine, (16, CHUNK, CO)), TILE, 0, 0, axis_index_groups=SPARSE, tiled=True
        )
    with jax.named_scope("gather_near"):
        near = lax.all_to_all(
            jnp.broadcast_to(far, (4, 16, CHUNK, CO)), TILE, 0, 0, axis_index_groups=BLOCKS, tiled=True
        )
    with jax.named_scope("order"):
        near = near.reshape(2, 2, 2, 2, 4, 7, CJ, CO)
        half = jnp.transpose(near, (2, 5, 3, 0, 4, 1, 6, 7)).reshape(14, CIN, CO)
    with jax.named_scope("swap"):
        other = lax.ppermute(half, "core", swap)
        first = jnp.where(core == 0, half, other)
        second = jnp.where(core == 0, other, half)
        order = [
            (first[0:3], first[9:12], second[0:3]),
            (first[3:6], first[12:14], second[9:10], second[3:6]),
            (first[6:9], second[10:13], second[6:9]),
        ]
        full = jnp.concatenate([piece for row_taps in order for piece in row_taps], axis=0)
        weight_grad = full.reshape(3, 3, 3, CIN, CO)
    with jax.named_scope("input_sum"):
        source = lax.broadcasted_iota(jnp.int32, (NZ, W, F * CI), 0)
        edges = shares[:, CHUNK:]
        above = jnp.sum(jnp.where(source < row, edges, 0.0), axis=0)
        below = jnp.sum(jnp.where(source > row, edges, 0.0), axis=0)
        total = inner.reshape(H, W, F * CI)
        total = jnp.concatenate([total[:1] + above, total[1:-1], total[-1:] + below], axis=0)
        total = total.astype(jnp.bfloat16).reshape(H, W, F, CI)
        input_grad = jnp.transpose(total, (2, 0, 1, 3))[None]
    return (input_grad, weight_grad)


def solution(mesh):
    grid = Mesh(mesh.devices.reshape(NZ, NY, NC, NX), AXES)
    in_specs = (
        P(TILE, None, None, None, "x"),
        P(TILE, None, None, None, "x"),
        P(None, None, None, None, "x"),
    )
    out_specs = (P(TILE, None, None, None, "x"), P(None, None, None, None, "x"))
    return jax.shard_map(shards, mesh=grid, in_specs=in_specs, out_specs=out_specs, check_vma=False)
```

```python
import math

import jax
import jax.numpy as jnp
from jax import lax
from jax.experimental import pallas as pl
from jax.experimental.pallas import tpu as pltpu
from jax.sharding import Mesh
from jax.sharding import PartitionSpec as P

AXES = ("z", "y", "core", "x")
TILE = ("z", "y", "core")
NZ, NY, NC, NX = 8, 8, 2, 4
F, H, W = 2, 8, 8
CIN, COUT = 256, 512
CI, CO = CIN // NX, COUT // NX
GROWS = F * H * W
EXT = (H + 2) * W
CJ = CI // NY
XROWS = 16
TERMS = 2 * EXT
CHUNK = 7 * CJ


def tile_index(z, y, core):
    return (z * NY + y) * NC + core


SPARSE = [
    [tile_index(a + 2 * i, b + 2 * j, c) for i in range(4) for j in range(4)]
    for a in range(2)
    for b in range(2)
    for c in range(NC)
]
BLOCKS = [
    [tile_index((2 * i + pz) % NZ, (2 * j + py) % NY, c) for pz in offsets for py in offsets]
    for i in range(NZ // 2)
    for j in range(NY // 2)
    for c, offsets in enumerate(((0, 1), (2, 1)))
]


def shifted(own, left, right, tap):
    if tap == 1:
        return own
    row = lax.broadcasted_iota(jnp.int32, own.shape, own.ndim - 2)
    axis = own.ndim - 2
    if tap == 0:
        return jnp.where(row == W - 1, pltpu.roll(right, W - 1, axis), pltpu.roll(own, W - 1, axis))
    return jnp.where(row == 0, pltpu.roll(left, 1, axis), pltpu.roll(own, 1, axis))


def input_kernel(col_ref, g_ref, k_ref, out_ref):
    col = col_ref[0]

    def tile(i):
        return g_ref[i, :GROWS, :].astype(jnp.float32).reshape(F * H, W, CO)

    own = tile(col)
    left = jnp.where(col > 0, tile(jnp.maximum(col - 1, 0)), 0.0)
    right = jnp.where(col < NY - 1, tile(jnp.minimum(col + 1, NY - 1)), 0.0)
    dims = (((1,), (1,)), ((), ()))
    sums = [[jnp.zeros((H * W, CIN), jnp.float32) for _ in range(3)] for _ in range(F)]
    for te in range(3):
        rows = shifted(own, left, right, te).reshape(F, H * W, CO).astype(jnp.bfloat16)
        both = jnp.concatenate([rows[0], rows[1]], axis=1)
        for tb in range(3):
            k0, k1, k2 = (k_ref[ta * 9 + tb * 3 + te] for ta in range(3))
            for f, pair in enumerate(((k1, k0), (k2, k1))):
                sums[f][tb] += lax.dot_general(
                    both, jnp.concatenate(pair, axis=1), dims, preferred_element_type=jnp.float32
                )
    tall = []
    for f in range(F):
        total = jnp.zeros((EXT, CIN), jnp.float32)
        for tb in range(3):
            parts = [sums[f][tb]]
            if tb > 0:
                parts.insert(0, jnp.zeros((tb * W, CIN), jnp.float32))
            if tb < 2:
                parts.append(jnp.zeros(((2 - tb) * W, CIN), jnp.float32))
            total += jnp.concatenate(parts, axis=0)
        tall.append(total)
    for i in range(NX):
        cut = slice(i * CI, (i + 1) * CI)
        value = jnp.concatenate([tall[0][:, cut], tall[1][:, cut]], axis=1)
        high = value.astype(jnp.bfloat16)
        out_ref[i, :EXT, :] = high
        out_ref[i, EXT:, :] = (value - high.astype(jnp.float32)).astype(jnp.bfloat16)


def split(prod):
    half = NX * CJ
    return prod[:half, CO:], prod[:half, :CO] + prod[half:, CO:], prod[half:, :CO]


def weight_kernel(place_ref, own_ref, pair_ref, got_ref, out_ref, inner_ref, edge_ref, mid_ref):
    core, row = place_ref[0], place_ref[1]
    terms = got_ref[:, :TERMS, :].astype(jnp.float32)
    terms = terms[:, :EXT, :] + terms[:, EXT:, :]
    terms = (terms[0] + terms[1]) + (terms[2] + terms[3])
    inner_ref[...] = terms[W : EXT - W]
    for z in range(NZ):
        up = jnp.where(row - 1 == z, terms[:W], 0.0)
        out_ref[z, CHUNK:, :] = jnp.where(row + 1 == z, terms[EXT - W :], up)

    x = got_ref[:, TERMS:, :].astype(jnp.float32)
    cell = lax.broadcasted_iota(jnp.int32, x.shape, 2) % (H * W)
    down = jnp.where(cell < W, 0.0, pltpu.roll(x, W, 2))
    up = jnp.where(cell >= (H - 1) * W, 0.0, pltpu.roll(x, F * H * W - W, 2))
    side = jnp.where(core == 0, down, up)
    shape = (NX, NC, NY, CJ, F * H * W)
    stack = []
    for value in (x.reshape(shape), side.reshape(shape)):
        for f in range(F):
            cut = slice(f * H * W, (f + 1) * H * W)
            cols = [
                value[:, clip, y, :, cut].reshape(NX * CJ, H * W)
                for clip in range(NC)
                for y in range(NY)
            ]
            stack.append(jnp.concatenate(cols, axis=1))
    xs = jnp.concatenate(stack, axis=0).astype(jnp.bfloat16)
    outer = x.reshape(shape)
    for f in range(F):
        first, last = f * H * W, (f + 1) * H * W - W
        cols = [
            jnp.where(
                core == 0,
                outer[:, clip, y, :, last : last + W],
                outer[:, clip, y, :, first : first + W],
            ).reshape(NX * CJ, W)
            for clip in range(NC)
            for y in range(NY)
        ]
        edge_ref[f * NX * CJ : (f + 1) * NX * CJ, :] = jnp.concatenate(cols, axis=1).astype(jnp.bfloat16)
    half = NX * CJ
    clips = [
        ref[:, :GROWS, :].astype(jnp.float32).reshape(NY, F * H, W, CO) for ref in (own_ref, pair_ref)
    ]
    border = jnp.zeros((1, F * H, W, CO), jnp.float32)

    def put(slot, value):
        group, t = divmod(slot, 7)
        for q in range(NX):
            out_ref[group * NX + q, t * CJ : (t + 1) * CJ, :] = value[q * CJ : (q + 1) * CJ]

    for te in range(3):
        cols = [[], []]
        for rows in clips:
            left = jnp.concatenate([border, rows[:-1]], axis=0)
            right = jnp.concatenate([rows[1:], border], axis=0)
            moved = shifted(rows, left, right, te).reshape(NY, F, H * W, CO)
            for f in range(F):
                cols[f].append(moved[:, f].reshape(NY * H * W, CO))
        both = [jnp.concatenate(c, axis=0).astype(jnp.bfloat16) for c in cols]
        prod = jnp.dot(xs, jnp.concatenate(both, axis=1), preferred_element_type=jnp.float32)
        for ta, value in enumerate(split(prod[: 2 * half])):
            mid_ref[ta * 3 + te] = value
        for ta, value in enumerate(split(prod[2 * half :])):
            put(ta * 3 + te, value)
    mid_ref[9] = jnp.zeros((half, CO), jnp.float32)
    for i in range(5):
        put(9 + i, mid_ref[i + 5 * core])


def edge_kernel(x_ref, g_ref, acc_ref, out_ref):
    out_ref[...] = acc_ref[...]
    border = jnp.zeros((1, F, W, CO), jnp.float32)
    for te in range(3):
        cols = [[], []]
        for clip in range(NC):
            rows = g_ref[clip].astype(jnp.float32)
            left = jnp.concatenate([border, rows[:-1]], axis=0)
            right = jnp.concatenate([rows[1:], border], axis=0)
            moved = shifted(rows, left, right, te)
            for f in range(F):
                cols[f].append(moved[:, f].reshape(NY * W, CO))
        both = [jnp.concatenate(c, axis=0).astype(jnp.bfloat16) for c in cols]
        prod = jnp.dot(x_ref[...], jnp.concatenate(both, axis=1), preferred_element_type=jnp.float32)
        for ta, value in enumerate(split(prod)):
            group, t = divmod(ta * 3 + te, 7)
            for q in range(NX):
                out_ref[group * NX + q, t * CJ : (t + 1) * CJ, :] += value[q * CJ : (q + 1) * CJ]


def shards(activations, out_grad, kernel):
    col = lax.axis_index("y").astype(jnp.int32)
    core = lax.axis_index("core").astype(jnp.int32)
    row = lax.axis_index("z").astype(jnp.int32)
    smem = pl.BlockSpec(memory_space=pltpu.SMEM)
    vmem = pl.BlockSpec(memory_space=pltpu.VMEM)
    params = pltpu.CompilerParams(vmem_limit_bytes=32 * 1024 * 1024)
    swap = [(0, 1), (1, 0)]
    with jax.named_scope("strip"):
        xt = activations[0].reshape(F * H * W, CI).T.reshape(NY, CJ, F * H * W)
        xt = jnp.pad(xt, ((0, 0), (0, XROWS - CJ), (0, 0)))
        rows = jnp.broadcast_to(out_grad[0].reshape(GROWS, CO), (NY, GROWS, CO))
        strip = lax.all_to_all(jnp.concatenate([rows, xt], axis=1), "y", 0, 0, tiled=True)
    with jax.named_scope("clips"):
        pair = lax.ppermute(strip, "core", swap)
    with jax.named_scope("input_part"):
        terms = pl.pallas_call(
            input_kernel,
            out_shape=jax.ShapeDtypeStruct((NX, TERMS, F * CI), jnp.bfloat16),
            in_specs=[smem, vmem, vmem],
            out_specs=vmem,
            compiler_params=params,
        )(col.reshape(1), strip, kernel.reshape(27, CIN, CO))
    with jax.named_scope("edges"):
        both = jnp.stack([strip[:, :GROWS], pair[:, :GROWS]]).reshape(NC, NY, F, H, W, CO)
        edge = jnp.where(core == 0, both[:, :, :, 0], both[:, :, :, H - 1])
        route = [(z * NC, (z - 1) * NC) for z in range(1, NZ)]
        route += [(z * NC + 1, (z + 1) * NC + 1) for z in range(NZ - 1)]
        edge = lax.ppermute(edge, ("z", "core"), route)
    with jax.named_scope("filters"):
        xmine = [s[:, GROWS : GROWS + CJ].reshape(NY * CJ, F * H * W) for s in (strip, pair)]
        xmine = jnp.broadcast_to(jnp.concatenate(xmine, axis=0), (NX, NC * NY * CJ, F * H * W))
        got = lax.all_to_all(jnp.concatenate([terms, xmine], axis=1), "x", 0, 0, tiled=True)
    with jax.named_scope("weight_part"):
        local, inner, outer = pl.pallas_call(
            weight_kernel,
            out_shape=[
                jax.ShapeDtypeStruct((NZ, CHUNK + W, CO), jnp.float32),
                jax.ShapeDtypeStruct((H * W, F * CI), jnp.float32),
                jax.ShapeDtypeStruct((F * NX * CJ, NC * NY * W), jnp.bfloat16),
            ],
            in_specs=[smem] + [vmem] * 3,
            out_specs=[vmem] * 3,
            scratch_shapes=[pltpu.VMEM((10, NX * CJ, CO), jnp.float32)],
            compiler_params=params,
        )(jnp.stack([core, row]), strip, pair, got)
    with jax.named_scope("weight_edge"):
        local = pl.pallas_call(
            edge_kernel,
            out_shape=jax.ShapeDtypeStruct(local.shape, jnp.float32),
            in_specs=[vmem] * 3,
            out_specs=vmem,
            input_output_aliases={2: 0},
            compiler_params=params,
        )(outer, edge, local)
    with jax.named_scope("weight_sum"):
        shares = lax.all_to_all(local, "z", 0, 0, tiled=True)
        scale = 1.0 / math.sqrt(NZ * NY * NC * F * H * W)
        mine = (jnp.sum(shares[:, :CHUNK], axis=0) * scale).astype(jnp.bfloat16)
    with jax.named_scope("gather_far"):
        far = lax.all_to_all(
            jnp.broadcast_to(mine, (16, CHUNK, CO)), TILE, 0, 0, axis_index_groups=SPARSE, tiled=True
        )
    with jax.named_scope("gather_near"):
        near = lax.all_to_all(
            jnp.broadcast_to(far, (4, 16, CHUNK, CO)), TILE, 0, 0, axis_index_groups=BLOCKS, tiled=True
        )
    with jax.named_scope("order"):
        near = near.reshape(2, 2, 2, 2, 4, 7, CJ, CO)
        half = jnp.transpose(near, (2, 5, 3, 0, 4, 1, 6, 7)).reshape(14, CIN, CO)
    with jax.named_scope("swap"):
        other = lax.ppermute(half, "core", swap)
        first = jnp.where(core == 0, half, other)
        second = jnp.where(core == 0, other, half)
        order = [
            (first[0:3], first[9:12], second[0:3]),
            (first[3:6], first[12:14], second[9:10], second[3:6]),
            (first[6:9], second[10:13], second[6:9]),
        ]
        full = jnp.concatenate([piece for row_taps in order for piece in row_taps], axis=0)
        weight_grad = full.reshape(3, 3, 3, CIN, CO)
    with jax.named_scope("input_sum"):
        source = lax.broadcasted_iota(jnp.int32, (NZ, W, F * CI), 0)
        edges = shares[:, CHUNK:]
        above = jnp.sum(jnp.where(source < row, edges, 0.0), axis=0)
        below = jnp.sum(jnp.where(source > row, edges, 0.0), axis=0)
        total = inner.reshape(H, W, F * CI)
        total = jnp.concatenate([total[:1] + above, total[1:-1], total[-1:] + below], axis=0)
        total = total.astype(jnp.bfloat16).reshape(H, W, F, CI)
        input_grad = jnp.transpose(total, (2, 0, 1, 3))[None]
    return (input_grad, weight_grad)


def solution(mesh):
    grid = Mesh(mesh.devices.reshape(NZ, NY, NC, NX), AXES)
    in_specs = (
        P(TILE, None, None, None, "x"),
        P(TILE, None, None, None, "x"),
        P(None, None, None, None, "x"),
    )
    out_specs = (P(TILE, None, None, None, "x"), P(None, None, None, None, "x"))
    return jax.shard_map(shards, mesh=grid, in_specs=in_specs, out_specs=out_specs, check_vma=False)
```

```python
import math

import jax
import jax.numpy as jnp
from jax import lax
from jax.experimental import pallas as pl
from jax.experimental.pallas import tpu as pltpu
from jax.sharding import Mesh
from jax.sharding import PartitionSpec as P

AXES = ("z", "y", "core", "x")
TILE = ("z", "y", "core")
NZ, NY, NC, NX = 8, 8, 2, 4
F, H, W = 2, 8, 8
CIN, COUT = 256, 512
CI, CO = CIN // NX, COUT // NX
GROWS = F * H * W
EXT = (H + 2) * W
CJ = CI // NY
XROWS = CJ
TERMS = 2 * EXT
CHUNK = 7 * CJ


def tile_index(z, y, core):
    return (z * NY + y) * NC + core


SPARSE = [
    [tile_index(a + 2 * i, b + 2 * j, c) for i in range(4) for j in range(4)]
    for a in range(2)
    for b in range(2)
    for c in range(NC)
]
BLOCKS = [
    [tile_index((2 * i + pz) % NZ, (2 * j + py) % NY, c) for pz in offsets for py in offsets]
    for i in range(NZ // 2)
    for j in range(NY // 2)
    for c, offsets in enumerate(((0, 1), (2, 1)))
]


def shifted(own, left, right, tap):
    if tap == 1:
        return own
    row = lax.broadcasted_iota(jnp.int32, own.shape, own.ndim - 2)
    axis = own.ndim - 2
    if tap == 0:
        return jnp.where(row == W - 1, pltpu.roll(right, W - 1, axis), pltpu.roll(own, W - 1, axis))
    return jnp.where(row == 0, pltpu.roll(left, 1, axis), pltpu.roll(own, 1, axis))


def input_kernel(col_ref, g_ref, k_ref, out_ref):
    col = col_ref[0]

    def tile(i):
        return g_ref[i, :GROWS, :].astype(jnp.float32).reshape(F * H, W, CO)

    own = tile(col)
    left = jnp.where(col > 0, tile(jnp.maximum(col - 1, 0)), 0.0)
    right = jnp.where(col < NY - 1, tile(jnp.minimum(col + 1, NY - 1)), 0.0)
    dims = (((1,), (1,)), ((), ()))
    sums = [[jnp.zeros((H * W, CIN), jnp.float32) for _ in range(3)] for _ in range(F)]
    for te in range(3):
        rows = shifted(own, left, right, te).reshape(F, H * W, CO).astype(jnp.bfloat16)
        both = jnp.concatenate([rows[0], rows[1]], axis=1)
        for tb in range(3):
            k0, k1, k2 = (k_ref[ta * 9 + tb * 3 + te] for ta in range(3))
            for f, pair in enumerate(((k1, k0), (k2, k1))):
                sums[f][tb] += lax.dot_general(
                    both, jnp.concatenate(pair, axis=1), dims, preferred_element_type=jnp.float32
                )
    tall = []
    for f in range(F):
        total = jnp.zeros((EXT, CIN), jnp.float32)
        for tb in range(3):
            parts = [sums[f][tb]]
            if tb > 0:
                parts.insert(0, jnp.zeros((tb * W, CIN), jnp.float32))
            if tb < 2:
                parts.append(jnp.zeros(((2 - tb) * W, CIN), jnp.float32))
            total += jnp.concatenate(parts, axis=0)
        tall.append(total)
    for i in range(NX):
        cut = slice(i * CI, (i + 1) * CI)
        value = jnp.concatenate([tall[0][:, cut], tall[1][:, cut]], axis=1)
        high = value.astype(jnp.bfloat16)
        out_ref[i, :EXT, :] = high
        out_ref[i, EXT:, :] = (value - high.astype(jnp.float32)).astype(jnp.bfloat16)


def split(prod):
    half = NX * CJ
    return prod[:half, CO:], prod[:half, :CO] + prod[half:, CO:], prod[half:, :CO]


def weight_kernel(place_ref, own_ref, pair_ref, got_ref, out_ref, inner_ref, edge_ref, mid_ref):
    core, row = place_ref[0], place_ref[1]
    terms = got_ref[:, :TERMS, :].astype(jnp.float32)
    terms = terms[:, :EXT, :] + terms[:, EXT:, :]
    terms = (terms[0] + terms[1]) + (terms[2] + terms[3])
    inner_ref[...] = terms[W : EXT - W]
    for z in range(NZ):
        up = jnp.where(row - 1 == z, terms[:W], 0.0)
        out_ref[z, CHUNK:, :] = jnp.where(row + 1 == z, terms[EXT - W :], up)

    x = got_ref[:, TERMS:, :].astype(jnp.float32)
    cell = lax.broadcasted_iota(jnp.int32, x.shape, 2) % (H * W)
    down = jnp.where(cell < W, 0.0, pltpu.roll(x, W, 2))
    up = jnp.where(cell >= (H - 1) * W, 0.0, pltpu.roll(x, F * H * W - W, 2))
    side = jnp.where(core == 0, down, up)
    shape = (NX, NC, NY, CJ, F * H * W)
    stack = []
    for value in (x.reshape(shape), side.reshape(shape)):
        for f in range(F):
            cut = slice(f * H * W, (f + 1) * H * W)
            cols = [
                value[:, clip, y, :, cut].reshape(NX * CJ, H * W)
                for clip in range(NC)
                for y in range(NY)
            ]
            stack.append(jnp.concatenate(cols, axis=1))
    xs = jnp.concatenate(stack, axis=0).astype(jnp.bfloat16)
    outer = x.reshape(shape)
    for f in range(F):
        first, last = f * H * W, (f + 1) * H * W - W
        cols = [
            jnp.where(
                core == 0,
                outer[:, clip, y, :, last : last + W],
                outer[:, clip, y, :, first : first + W],
            ).reshape(NX * CJ, W)
            for clip in range(NC)
            for y in range(NY)
        ]
        edge_ref[f * NX * CJ : (f + 1) * NX * CJ, :] = jnp.concatenate(cols, axis=1).astype(jnp.bfloat16)
    half = NX * CJ
    clips = [
        ref[:, :GROWS, :].astype(jnp.float32).reshape(NY, F * H, W, CO) for ref in (own_ref, pair_ref)
    ]
    border = jnp.zeros((1, F * H, W, CO), jnp.float32)

    def put(slot, value):
        group, t = divmod(slot, 7)
        for q in range(NX):
            out_ref[group * NX + q, t * CJ : (t + 1) * CJ, :] = value[q * CJ : (q + 1) * CJ]

    for te in range(3):
        cols = [[], []]
        for rows in clips:
            left = jnp.concatenate([border, rows[:-1]], axis=0)
            right = jnp.concatenate([rows[1:], border], axis=0)
            moved = shifted(rows, left, right, te).reshape(NY, F, H * W, CO)
            for f in range(F):
                cols[f].append(moved[:, f].reshape(NY * H * W, CO))
        both = [jnp.concatenate(c, axis=0).astype(jnp.bfloat16) for c in cols]
        prod = jnp.dot(xs, jnp.concatenate(both, axis=1), preferred_element_type=jnp.float32)
        for ta, value in enumerate(split(prod[: 2 * half])):
            mid_ref[ta * 3 + te] = value
        for ta, value in enumerate(split(prod[2 * half :])):
            put(ta * 3 + te, value)
    mid_ref[9] = jnp.zeros((half, CO), jnp.float32)
    for i in range(5):
        put(9 + i, mid_ref[i + 5 * core])


def edge_kernel(x_ref, g_ref, acc_ref, out_ref):
    out_ref[...] = acc_ref[...]
    border = jnp.zeros((1, F, W, CO), jnp.float32)
    for te in range(3):
        cols = [[], []]
        for clip in range(NC):
            rows = g_ref[clip].astype(jnp.float32)
            left = jnp.concatenate([border, rows[:-1]], axis=0)
            right = jnp.concatenate([rows[1:], border], axis=0)
            moved = shifted(rows, left, right, te)
            for f in range(F):
                cols[f].append(moved[:, f].reshape(NY * W, CO))
        both = [jnp.concatenate(c, axis=0).astype(jnp.bfloat16) for c in cols]
        prod = jnp.dot(x_ref[...], jnp.concatenate(both, axis=1), preferred_element_type=jnp.float32)
        for ta, value in enumerate(split(prod)):
            group, t = divmod(ta * 3 + te, 7)
            for q in range(NX):
                out_ref[group * NX + q, t * CJ : (t + 1) * CJ, :] += value[q * CJ : (q + 1) * CJ]


def shards(activations, out_grad, kernel):
    col = lax.axis_index("y").astype(jnp.int32)
    core = lax.axis_index("core").astype(jnp.int32)
    row = lax.axis_index("z").astype(jnp.int32)
    smem = pl.BlockSpec(memory_space=pltpu.SMEM)
    vmem = pl.BlockSpec(memory_space=pltpu.VMEM)
    params = pltpu.CompilerParams(vmem_limit_bytes=32 * 1024 * 1024)
    swap = [(0, 1), (1, 0)]
    with jax.named_scope("strip"):
        xt = activations[0].reshape(F * H * W, CI).T.reshape(NY, CJ, F * H * W)
        xt = jnp.pad(xt, ((0, 0), (0, XROWS - CJ), (0, 0)))
        rows = jnp.broadcast_to(out_grad[0].reshape(GROWS, CO), (NY, GROWS, CO))
        strip = lax.all_to_all(jnp.concatenate([rows, xt], axis=1), "y", 0, 0, tiled=True)
    with jax.named_scope("clips"):
        pair = lax.ppermute(strip, "core", swap)
    with jax.named_scope("input_part"):
        terms = pl.pallas_call(
            input_kernel,
            out_shape=jax.ShapeDtypeStruct((NX, TERMS, F * CI), jnp.bfloat16),
            in_specs=[smem, vmem, vmem],
            out_specs=vmem,
            compiler_params=params,
        )(col.reshape(1), strip, kernel.reshape(27, CIN, CO))
    with jax.named_scope("edges"):
        both = jnp.stack([strip[:, :GROWS], pair[:, :GROWS]]).reshape(NC, NY, F, H, W, CO)
        edge = jnp.where(core == 0, both[:, :, :, 0], both[:, :, :, H - 1])
        route = [(z * NC, (z - 1) * NC) for z in range(1, NZ)]
        route += [(z * NC + 1, (z + 1) * NC + 1) for z in range(NZ - 1)]
        edge = lax.ppermute(edge, ("z", "core"), route)
    with jax.named_scope("filters"):
        xmine = [s[:, GROWS : GROWS + CJ].reshape(NY * CJ, F * H * W) for s in (strip, pair)]
        xmine = jnp.broadcast_to(jnp.concatenate(xmine, axis=0), (NX, NC * NY * CJ, F * H * W))
        got = lax.all_to_all(jnp.concatenate([terms, xmine], axis=1), "x", 0, 0, tiled=True)
    with jax.named_scope("weight_part"):
        local, inner, outer = pl.pallas_call(
            weight_kernel,
            out_shape=[
                jax.ShapeDtypeStruct((NZ, CHUNK + W, CO), jnp.float32),
                jax.ShapeDtypeStruct((H * W, F * CI), jnp.float32),
                jax.ShapeDtypeStruct((F * NX * CJ, NC * NY * W), jnp.bfloat16),
            ],
            in_specs=[smem] + [vmem] * 3,
            out_specs=[vmem] * 3,
            scratch_shapes=[pltpu.VMEM((10, NX * CJ, CO), jnp.float32)],
            compiler_params=params,
        )(jnp.stack([core, row]), strip, pair, got)
    with jax.named_scope("weight_edge"):
        local = pl.pallas_call(
            edge_kernel,
            out_shape=jax.ShapeDtypeStruct(local.shape, jnp.float32),
            in_specs=[vmem] * 3,
            out_specs=vmem,
            input_output_aliases={2: 0},
            compiler_params=params,
        )(outer, edge, local)
    with jax.named_scope("weight_sum"):
        shares = lax.all_to_all(local, "z", 0, 0, tiled=True)
        scale = 1.0 / math.sqrt(NZ * NY * NC * F * H * W)
        mine = (jnp.sum(shares[:, :CHUNK], axis=0) * scale).astype(jnp.bfloat16)
    with jax.named_scope("gather_far"):
        far = lax.all_to_all(
            jnp.broadcast_to(mine, (16, CHUNK, CO)), TILE, 0, 0, axis_index_groups=SPARSE, tiled=True
        )
    with jax.named_scope("gather_near"):
        near = lax.all_to_all(
            jnp.broadcast_to(far, (4, 16, CHUNK, CO)), TILE, 0, 0, axis_index_groups=BLOCKS, tiled=True
        )
    with jax.named_scope("order"):
        near = near.reshape(2, 2, 2, 2, 4, 7, CJ, CO)
        half = jnp.transpose(near, (2, 5, 3, 0, 4, 1, 6, 7)).reshape(14, CIN, CO)
    with jax.named_scope("swap"):
        other = lax.ppermute(half, "core", swap)
        first = jnp.where(core == 0, half, other)
        second = jnp.where(core == 0, other, half)
        order = [
            (first[0:3], first[9:12], second[0:3]),
            (first[3:6], first[12:14], second[9:10], second[3:6]),
            (first[6:9], second[10:13], second[6:9]),
        ]
        full = jnp.concatenate([piece for row_taps in order for piece in row_taps], axis=0)
        weight_grad = full.reshape(3, 3, 3, CIN, CO)
    with jax.named_scope("input_sum"):
        source = lax.broadcasted_iota(jnp.int32, (NZ, W, F * CI), 0)
        edges = shares[:, CHUNK:]
        above = jnp.sum(jnp.where(source < row, edges, 0.0), axis=0)
        below = jnp.sum(jnp.where(source > row, edges, 0.0), axis=0)
        total = inner.reshape(H, W, F * CI)
        total = jnp.concatenate([total[:1] + above, total[1:-1], total[-1:] + below], axis=0)
        total = total.astype(jnp.bfloat16).reshape(H, W, F, CI)
        input_grad = jnp.transpose(total, (2, 0, 1, 3))[None]
    return (input_grad, weight_grad)


def solution(mesh):
    grid = Mesh(mesh.devices.reshape(NZ, NY, NC, NX), AXES)
    in_specs = (
        P(TILE, None, None, None, "x"),
        P(TILE, None, None, None, "x"),
        P(None, None, None, None, "x"),
    )
    out_specs = (P(TILE, None, None, None, "x"), P(None, None, None, None, "x"))
    return jax.shard_map(shards, mesh=grid, in_specs=in_specs, out_specs=out_specs, check_vma=False)
```

```python
import math

import jax
import jax.numpy as jnp
from jax import lax
from jax.experimental import pallas as pl
from jax.experimental.pallas import tpu as pltpu
from jax.sharding import Mesh
from jax.sharding import PartitionSpec as P

AXES = ("z", "y", "core", "x")
TILE = ("z", "y", "core")
NZ, NY, NC, NX = 8, 8, 2, 4
F, H, W = 2, 8, 8
CIN, COUT = 256, 512
CI, CO = CIN // NX, COUT // NX
GROWS = F * H * W
EXT = (H + 2) * W
CJ = CI // NY
XROWS = CJ
TERMS = 2 * EXT
CHUNK = 7 * CJ


def tile_index(z, y, core):
    return (z * NY + y) * NC + core


SPARSE = [
    [tile_index(a + 2 * i, b + 2 * j, c) for i in range(4) for j in range(4)]
    for a in range(2)
    for b in range(2)
    for c in range(NC)
]
BLOCKS = [
    [tile_index((2 * i + pz) % NZ, (2 * j + py) % NY, c) for pz in offsets for py in offsets]
    for i in range(NZ // 2)
    for j in range(NY // 2)
    for c, offsets in enumerate(((0, 1), (2, 1)))
]


def shifted(own, left, right, tap):
    if tap == 1:
        return own
    row = lax.broadcasted_iota(jnp.int32, own.shape, own.ndim - 2)
    axis = own.ndim - 2
    if tap == 0:
        return jnp.where(row == W - 1, pltpu.roll(right, W - 1, axis), pltpu.roll(own, W - 1, axis))
    return jnp.where(row == 0, pltpu.roll(left, 1, axis), pltpu.roll(own, 1, axis))


def input_kernel(col_ref, g_ref, k_hbm, out_ref, k_ref, sems):
    col = col_ref[0]
    copies = [
        pltpu.make_async_copy(k_hbm.at[pl.ds(9 * ta, 9)], k_ref.at[pl.ds(9 * ta, 9)], sems.at[ta])
        for ta in range(3)
    ]
    for copy in copies:
        copy.start()

    def tile(i):
        return g_ref[i, :GROWS, :].astype(jnp.float32).reshape(F * H, W, CO)

    own = tile(col)
    left = jnp.where(col > 0, tile(jnp.maximum(col - 1, 0)), 0.0)
    right = jnp.where(col < NY - 1, tile(jnp.minimum(col + 1, NY - 1)), 0.0)
    dims = (((1,), (1,)), ((), ()))
    sums = [[jnp.zeros((H * W, CIN), jnp.float32) for _ in range(3)] for _ in range(F)]
    for copy in copies:
        copy.wait()
    for te in range(3):
        rows = shifted(own, left, right, te).reshape(F, H * W, CO).astype(jnp.bfloat16)
        both = jnp.concatenate([rows[0], rows[1]], axis=1)
        for tb in range(3):
            k0, k1, k2 = (k_ref[ta * 9 + tb * 3 + te] for ta in range(3))
            for f, pair in enumerate(((k1, k0), (k2, k1))):
                sums[f][tb] += lax.dot_general(
                    both, jnp.concatenate(pair, axis=1), dims, preferred_element_type=jnp.float32
                )
    tall = []
    for f in range(F):
        total = jnp.zeros((EXT, CIN), jnp.float32)
        for tb in range(3):
            parts = [sums[f][tb]]
            if tb > 0:
                parts.insert(0, jnp.zeros((tb * W, CIN), jnp.float32))
            if tb < 2:
                parts.append(jnp.zeros(((2 - tb) * W, CIN), jnp.float32))
            total += jnp.concatenate(parts, axis=0)
        tall.append(total)
    for i in range(NX):
        cut = slice(i * CI, (i + 1) * CI)
        value = jnp.concatenate([tall[0][:, cut], tall[1][:, cut]], axis=1)
        high = value.astype(jnp.bfloat16)
        out_ref[i, :EXT, :] = high
        out_ref[i, EXT:, :] = (value - high.astype(jnp.float32)).astype(jnp.bfloat16)


def split(prod):
    half = NX * CJ
    return prod[:half, CO:], prod[:half, :CO] + prod[half:, CO:], prod[half:, :CO]


def weight_kernel(place_ref, own_ref, pair_ref, got_ref, out_ref, inner_ref, edge_ref, mid_ref):
    core, row = place_ref[0], place_ref[1]
    terms = got_ref[:, :TERMS, :].astype(jnp.float32)
    terms = terms[:, :EXT, :] + terms[:, EXT:, :]
    terms = (terms[0] + terms[1]) + (terms[2] + terms[3])
    inner_ref[...] = terms[W : EXT - W]
    for z in range(NZ):
        up = jnp.where(row - 1 == z, terms[:W], 0.0)
        out_ref[z, CHUNK:, :] = jnp.where(row + 1 == z, terms[EXT - W :], up)

    x = got_ref[:, TERMS:, :].astype(jnp.float32)
    cell = lax.broadcasted_iota(jnp.int32, x.shape, 2) % (H * W)
    down = jnp.where(cell < W, 0.0, pltpu.roll(x, W, 2))
    up = jnp.where(cell >= (H - 1) * W, 0.0, pltpu.roll(x, F * H * W - W, 2))
    side = jnp.where(core == 0, down, up)
    shape = (NX, NC, NY, CJ, F * H * W)
    stack = []
    for value in (x.reshape(shape), side.reshape(shape)):
        for f in range(F):
            cut = slice(f * H * W, (f + 1) * H * W)
            cols = [
                value[:, clip, y, :, cut].reshape(NX * CJ, H * W)
                for clip in range(NC)
                for y in range(NY)
            ]
            stack.append(jnp.concatenate(cols, axis=1))
    xs = jnp.concatenate(stack, axis=0).astype(jnp.bfloat16)
    outer = x.reshape(shape)
    for f in range(F):
        first, last = f * H * W, (f + 1) * H * W - W
        cols = [
            jnp.where(
                core == 0,
                outer[:, clip, y, :, last : last + W],
                outer[:, clip, y, :, first : first + W],
            ).reshape(NX * CJ, W)
            for clip in range(NC)
            for y in range(NY)
        ]
        edge_ref[f * NX * CJ : (f + 1) * NX * CJ, :] = jnp.concatenate(cols, axis=1).astype(jnp.bfloat16)
    half = NX * CJ
    clips = [
        ref[:, :GROWS, :].astype(jnp.float32).reshape(NY, F * H, W, CO) for ref in (own_ref, pair_ref)
    ]
    border = jnp.zeros((1, F * H, W, CO), jnp.float32)

    def put(slot, value):
        group, t = divmod(slot, 7)
        for q in range(NX):
            out_ref[group * NX + q, t * CJ : (t + 1) * CJ, :] = value[q * CJ : (q + 1) * CJ]

    for te in range(3):
        cols = [[], []]
        for rows in clips:
            left = jnp.concatenate([border, rows[:-1]], axis=0)
            right = jnp.concatenate([rows[1:], border], axis=0)
            moved = shifted(rows, left, right, te).reshape(NY, F, H * W, CO)
            for f in range(F):
                cols[f].append(moved[:, f].reshape(NY * H * W, CO))
        both = [jnp.concatenate(c, axis=0).astype(jnp.bfloat16) for c in cols]
        prod = jnp.dot(xs, jnp.concatenate(both, axis=1), preferred_element_type=jnp.float32)
        for ta, value in enumerate(split(prod[: 2 * half])):
            mid_ref[ta * 3 + te] = value
        for ta, value in enumerate(split(prod[2 * half :])):
            put(ta * 3 + te, value)
    mid_ref[9] = jnp.zeros((half, CO), jnp.float32)
    for i in range(5):
        put(9 + i, mid_ref[i + 5 * core])


def edge_kernel(x_ref, g_ref, acc_ref, out_ref):
    out_ref[...] = acc_ref[...]
    border = jnp.zeros((1, F, W, CO), jnp.float32)
    for te in range(3):
        cols = [[], []]
        for clip in range(NC):
            rows = g_ref[clip].astype(jnp.float32)
            left = jnp.concatenate([border, rows[:-1]], axis=0)
            right = jnp.concatenate([rows[1:], border], axis=0)
            moved = shifted(rows, left, right, te)
            for f in range(F):
                cols[f].append(moved[:, f].reshape(NY * W, CO))
        both = [jnp.concatenate(c, axis=0).astype(jnp.bfloat16) for c in cols]
        prod = jnp.dot(x_ref[...], jnp.concatenate(both, axis=1), preferred_element_type=jnp.float32)
        for ta, value in enumerate(split(prod)):
            group, t = divmod(ta * 3 + te, 7)
            for q in range(NX):
                out_ref[group * NX + q, t * CJ : (t + 1) * CJ, :] += value[q * CJ : (q + 1) * CJ]


def shards(activations, out_grad, kernel):
    col = lax.axis_index("y").astype(jnp.int32)
    core = lax.axis_index("core").astype(jnp.int32)
    row = lax.axis_index("z").astype(jnp.int32)
    smem = pl.BlockSpec(memory_space=pltpu.SMEM)
    vmem = pl.BlockSpec(memory_space=pltpu.VMEM)
    params = pltpu.CompilerParams(vmem_limit_bytes=32 * 1024 * 1024)
    swap = [(0, 1), (1, 0)]
    with jax.named_scope("strip"):
        xt = activations[0].reshape(F * H * W, CI).T.reshape(NY, CJ, F * H * W)
        xt = jnp.pad(xt, ((0, 0), (0, XROWS - CJ), (0, 0)))
        rows = jnp.broadcast_to(out_grad[0].reshape(GROWS, CO), (NY, GROWS, CO))
        strip = lax.all_to_all(jnp.concatenate([rows, xt], axis=1), "y", 0, 0, tiled=True)
    with jax.named_scope("clips"):
        pair = lax.ppermute(strip, "core", swap)
    with jax.named_scope("input_part"):
        terms = pl.pallas_call(
            input_kernel,
            out_shape=jax.ShapeDtypeStruct((NX, TERMS, F * CI), jnp.bfloat16),
            in_specs=[smem, vmem, pl.BlockSpec(memory_space=pltpu.HBM)],
            out_specs=vmem,
            scratch_shapes=[pltpu.VMEM((27, CIN, CO), jnp.bfloat16), pltpu.SemaphoreType.DMA((3,))],
            compiler_params=params,
        )(col.reshape(1), strip, kernel.reshape(27, CIN, CO))
    with jax.named_scope("edges"):
        both = jnp.stack([strip[:, :GROWS], pair[:, :GROWS]]).reshape(NC, NY, F, H, W, CO)
        edge = jnp.where(core == 0, both[:, :, :, 0], both[:, :, :, H - 1])
        route = [(z * NC, (z - 1) * NC) for z in range(1, NZ)]
        route += [(z * NC + 1, (z + 1) * NC + 1) for z in range(NZ - 1)]
        edge = lax.ppermute(edge, ("z", "core"), route)
    with jax.named_scope("filters"):
        xmine = [s[:, GROWS : GROWS + CJ].reshape(NY * CJ, F * H * W) for s in (strip, pair)]
        xmine = jnp.broadcast_to(jnp.concatenate(xmine, axis=0), (NX, NC * NY * CJ, F * H * W))
        got = lax.all_to_all(jnp.concatenate([terms, xmine], axis=1), "x", 0, 0, tiled=True)
    with jax.named_scope("weight_part"):
        local, inner, outer = pl.pallas_call(
            weight_kernel,
            out_shape=[
                jax.ShapeDtypeStruct((NZ, CHUNK + W, CO), jnp.float32),
                jax.ShapeDtypeStruct((H * W, F * CI), jnp.float32),
                jax.ShapeDtypeStruct((F * NX * CJ, NC * NY * W), jnp.bfloat16),
            ],
            in_specs=[smem] + [vmem] * 3,
            out_specs=[vmem] * 3,
            scratch_shapes=[pltpu.VMEM((10, NX * CJ, CO), jnp.float32)],
            compiler_params=params,
        )(jnp.stack([core, row]), strip, pair, got)
    with jax.named_scope("weight_edge"):
        local = pl.pallas_call(
            edge_kernel,
            out_shape=jax.ShapeDtypeStruct(local.shape, jnp.float32),
            in_specs=[vmem] * 3,
            out_specs=vmem,
            input_output_aliases={2: 0},
            compiler_params=params,
        )(outer, edge, local)
    with jax.named_scope("weight_sum"):
        shares = lax.all_to_all(local, "z", 0, 0, tiled=True)
        scale = 1.0 / math.sqrt(NZ * NY * NC * F * H * W)
        mine = (jnp.sum(shares[:, :CHUNK], axis=0) * scale).astype(jnp.bfloat16)
    with jax.named_scope("gather_far"):
        far = lax.all_to_all(
            jnp.broadcast_to(mine, (16, CHUNK, CO)), TILE, 0, 0, axis_index_groups=SPARSE, tiled=True
        )
    with jax.named_scope("gather_near"):
        near = lax.all_to_all(
            jnp.broadcast_to(far, (4, 16, CHUNK, CO)), TILE, 0, 0, axis_index_groups=BLOCKS, tiled=True
        )
    with jax.named_scope("order"):
        near = near.reshape(2, 2, 2, 2, 4, 7, CJ, CO)
        half = jnp.transpose(near, (2, 5, 3, 0, 4, 1, 6, 7)).reshape(14, CIN, CO)
    with jax.named_scope("swap"):
        other = lax.ppermute(half, "core", swap)
        first = jnp.where(core == 0, half, other)
        second = jnp.where(core == 0, other, half)
        order = [
            (first[0:3], first[9:12], second[0:3]),
            (first[3:6], first[12:14], second[9:10], second[3:6]),
            (first[6:9], second[10:13], second[6:9]),
        ]
        full = jnp.concatenate([piece for row_taps in order for piece in row_taps], axis=0)
        weight_grad = full.reshape(3, 3, 3, CIN, CO)
    with jax.named_scope("input_sum"):
        source = lax.broadcasted_iota(jnp.int32, (NZ, W, F * CI), 0)
        edges = shares[:, CHUNK:]
        above = jnp.sum(jnp.where(source < row, edges, 0.0), axis=0)
        below = jnp.sum(jnp.where(source > row, edges, 0.0), axis=0)
        total = inner.reshape(H, W, F * CI)
        total = jnp.concatenate([total[:1] + above, total[1:-1], total[-1:] + below], axis=0)
        total = total.astype(jnp.bfloat16).reshape(H, W, F, CI)
        input_grad = jnp.transpose(total, (2, 0, 1, 3))[None]
    return (input_grad, weight_grad)


def solution(mesh):
    grid = Mesh(mesh.devices.reshape(NZ, NY, NC, NX), AXES)
    in_specs = (
        P(TILE, None, None, None, "x"),
        P(TILE, None, None, None, "x"),
        P(None, None, None, None, "x"),
    )
    out_specs = (P(TILE, None, None, None, "x"), P(None, None, None, None, "x"))
    return jax.shard_map(shards, mesh=grid, in_specs=in_specs, out_specs=out_specs, check_vma=False)
```

```python
import math

import jax
import jax.numpy as jnp
from jax import lax
from jax.experimental import pallas as pl
from jax.experimental.pallas import tpu as pltpu
from jax.sharding import Mesh
from jax.sharding import PartitionSpec as P

AXES = ("z", "y", "core", "x")
TILE = ("z", "y", "core")
NZ, NY, NC, NX = 8, 8, 2, 4
F, H, W = 2, 8, 8
CIN, COUT = 256, 512
CI, CO = CIN // NX, COUT // NX
GROWS = F * H * W
EXT = (H + 2) * W
CJ = CI // NY
XROWS = CJ
TERMS = 2 * EXT
CHUNK = 7 * CJ


def tile_index(z, y, core):
    return (z * NY + y) * NC + core


SPARSE = [
    [tile_index(a + 2 * i, b + 2 * j, c) for i in range(4) for j in range(4)]
    for a in range(2)
    for b in range(2)
    for c in range(NC)
]
BLOCKS = [
    [tile_index((2 * i + pz) % NZ, (2 * j + py) % NY, c) for pz in offsets for py in offsets]
    for i in range(NZ // 2)
    for j in range(NY // 2)
    for c, offsets in enumerate(((0, 1), (2, 1)))
]


def shifted(own, left, right, tap):
    if tap == 1:
        return own
    row = lax.broadcasted_iota(jnp.int32, own.shape, own.ndim - 2)
    axis = own.ndim - 2
    if tap == 0:
        return jnp.where(row == W - 1, pltpu.roll(right, W - 1, axis), pltpu.roll(own, W - 1, axis))
    return jnp.where(row == 0, pltpu.roll(left, 1, axis), pltpu.roll(own, 1, axis))


def input_kernel(col_ref, g_ref, k_ref, out_ref):
    col = col_ref[0]

    def tile(i):
        return g_ref[i, :GROWS, :].astype(jnp.float32).reshape(F * H, W, CO)

    own = tile(col)
    left = jnp.where(col > 0, tile(jnp.maximum(col - 1, 0)), 0.0)
    right = jnp.where(col < NY - 1, tile(jnp.minimum(col + 1, NY - 1)), 0.0)
    dims = (((1,), (1,)), ((), ()))
    sums = [[jnp.zeros((H * W, CIN), jnp.float32) for _ in range(3)] for _ in range(F)]
    for te in range(3):
        rows = shifted(own, left, right, te).reshape(F, H * W, CO).astype(jnp.bfloat16)
        both = jnp.concatenate([rows[0], rows[1]], axis=1)
        for tb in range(3):
            k0, k1, k2 = (k_ref[ta * 9 + tb * 3 + te] for ta in range(3))
            for f, pair in enumerate(((k1, k0), (k2, k1))):
                sums[f][tb] += lax.dot_general(
                    both, jnp.concatenate(pair, axis=1), dims, preferred_element_type=jnp.float32
                )
    tall = []
    for f in range(F):
        total = jnp.zeros((EXT, CIN), jnp.float32)
        for tb in range(3):
            parts = [sums[f][tb]]
            if tb > 0:
                parts.insert(0, jnp.zeros((tb * W, CIN), jnp.float32))
            if tb < 2:
                parts.append(jnp.zeros(((2 - tb) * W, CIN), jnp.float32))
            total += jnp.concatenate(parts, axis=0)
        tall.append(total)
    for i in range(NX):
        cut = slice(i * CI, (i + 1) * CI)
        value = jnp.concatenate([tall[0][:, cut], tall[1][:, cut]], axis=1)
        high = value.astype(jnp.bfloat16)
        out_ref[i, :EXT, :] = high
        out_ref[i, EXT:, :] = (value - high.astype(jnp.float32)).astype(jnp.bfloat16)


def split(prod):
    half = NX * CJ
    return prod[:half, CO:], prod[:half, :CO] + prod[half:, CO:], prod[half:, :CO]


def weight_kernel(place_ref, own_ref, pair_ref, got_ref, out_ref, edge_ref, mid_ref):
    core, row = place_ref[0], place_ref[1]
    terms = got_ref[:, :TERMS, :].astype(jnp.float32)

    def total(start):
        part = terms[:, start : start + W] + terms[:, EXT + start : EXT + start + W]
        return (part[0] + part[1]) + (part[2] + part[3])

    above, below = total(0), total(EXT - W)
    for z in range(NZ):
        up = jnp.where(row - 1 == z, above, 0.0)
        out_ref[z, CHUNK:, :] = jnp.where(row + 1 == z, below, up)

    x = got_ref[:, TERMS:, :].astype(jnp.float32)
    cell = lax.broadcasted_iota(jnp.int32, x.shape, 2) % (H * W)
    down = jnp.where(cell < W, 0.0, pltpu.roll(x, W, 2))
    up = jnp.where(cell >= (H - 1) * W, 0.0, pltpu.roll(x, F * H * W - W, 2))
    side = jnp.where(core == 0, down, up)
    shape = (NX, NC, NY, CJ, F * H * W)
    stack = []
    for value in (x.reshape(shape), side.reshape(shape)):
        for f in range(F):
            cut = slice(f * H * W, (f + 1) * H * W)
            cols = [
                value[:, clip, y, :, cut].reshape(NX * CJ, H * W)
                for clip in range(NC)
                for y in range(NY)
            ]
            stack.append(jnp.concatenate(cols, axis=1))
    xs = jnp.concatenate(stack, axis=0).astype(jnp.bfloat16)
    outer = x.reshape(shape)
    for f in range(F):
        first, last = f * H * W, (f + 1) * H * W - W
        cols = [
            jnp.where(
                core == 0,
                outer[:, clip, y, :, last : last + W],
                outer[:, clip, y, :, first : first + W],
            ).reshape(NX * CJ, W)
            for clip in range(NC)
            for y in range(NY)
        ]
        edge_ref[f * NX * CJ : (f + 1) * NX * CJ, :] = jnp.concatenate(cols, axis=1).astype(jnp.bfloat16)
    half = NX * CJ
    clips = [
        ref[:, :GROWS, :].astype(jnp.float32).reshape(NY, F * H, W, CO) for ref in (own_ref, pair_ref)
    ]
    border = jnp.zeros((1, F * H, W, CO), jnp.float32)

    def put(slot, value):
        group, t = divmod(slot, 7)
        for q in range(NX):
            out_ref[group * NX + q, t * CJ : (t + 1) * CJ, :] = value[q * CJ : (q + 1) * CJ]

    for te in range(3):
        cols = [[], []]
        for rows in clips:
            left = jnp.concatenate([border, rows[:-1]], axis=0)
            right = jnp.concatenate([rows[1:], border], axis=0)
            moved = shifted(rows, left, right, te).reshape(NY, F, H * W, CO)
            for f in range(F):
                cols[f].append(moved[:, f].reshape(NY * H * W, CO))
        both = [jnp.concatenate(c, axis=0).astype(jnp.bfloat16) for c in cols]
        prod = jnp.dot(xs, jnp.concatenate(both, axis=1), preferred_element_type=jnp.float32)
        for ta, value in enumerate(split(prod[: 2 * half])):
            mid_ref[ta * 3 + te] = value
        for ta, value in enumerate(split(prod[2 * half :])):
            put(ta * 3 + te, value)
    mid_ref[9] = jnp.zeros((half, CO), jnp.float32)
    for i in range(5):
        put(9 + i, mid_ref[i + 5 * core])


def edge_kernel(x_ref, g_ref, acc_ref, out_ref):
    out_ref[...] = acc_ref[...]
    border = jnp.zeros((1, F, W, CO), jnp.float32)
    for te in range(3):
        cols = [[], []]
        for clip in range(NC):
            rows = g_ref[clip].astype(jnp.float32)
            left = jnp.concatenate([border, rows[:-1]], axis=0)
            right = jnp.concatenate([rows[1:], border], axis=0)
            moved = shifted(rows, left, right, te)
            for f in range(F):
                cols[f].append(moved[:, f].reshape(NY * W, CO))
        both = [jnp.concatenate(c, axis=0).astype(jnp.bfloat16) for c in cols]
        prod = jnp.dot(x_ref[...], jnp.concatenate(both, axis=1), preferred_element_type=jnp.float32)
        for ta, value in enumerate(split(prod)):
            group, t = divmod(ta * 3 + te, 7)
            for q in range(NX):
                out_ref[group * NX + q, t * CJ : (t + 1) * CJ, :] += value[q * CJ : (q + 1) * CJ]


def shards(activations, out_grad, kernel):
    col = lax.axis_index("y").astype(jnp.int32)
    core = lax.axis_index("core").astype(jnp.int32)
    row = lax.axis_index("z").astype(jnp.int32)
    smem = pl.BlockSpec(memory_space=pltpu.SMEM)
    vmem = pl.BlockSpec(memory_space=pltpu.VMEM)
    params = pltpu.CompilerParams(vmem_limit_bytes=32 * 1024 * 1024)
    swap = [(0, 1), (1, 0)]
    with jax.named_scope("strip"):
        xt = activations[0].reshape(F * H * W, CI).T.reshape(NY, CJ, F * H * W)
        xt = jnp.pad(xt, ((0, 0), (0, XROWS - CJ), (0, 0)))
        rows = jnp.broadcast_to(out_grad[0].reshape(GROWS, CO), (NY, GROWS, CO))
        strip = lax.all_to_all(jnp.concatenate([rows, xt], axis=1), "y", 0, 0, tiled=True)
    with jax.named_scope("clips"):
        pair = lax.ppermute(strip, "core", swap)
    with jax.named_scope("input_part"):
        terms = pl.pallas_call(
            input_kernel,
            out_shape=jax.ShapeDtypeStruct((NX, TERMS, F * CI), jnp.bfloat16),
            in_specs=[smem, vmem, vmem],
            out_specs=vmem,
            compiler_params=params,
        )(col.reshape(1), strip, kernel.reshape(27, CIN, CO))
    with jax.named_scope("edges"):
        both = jnp.stack([strip[:, :GROWS], pair[:, :GROWS]]).reshape(NC, NY, F, H, W, CO)
        edge = jnp.where(core == 0, both[:, :, :, 0], both[:, :, :, H - 1])
        route = [(z * NC, (z - 1) * NC) for z in range(1, NZ)]
        route += [(z * NC + 1, (z + 1) * NC + 1) for z in range(NZ - 1)]
        edge = lax.ppermute(edge, ("z", "core"), route)
    with jax.named_scope("filters"):
        xmine = [s[:, GROWS : GROWS + CJ].reshape(NY * CJ, F * H * W) for s in (strip, pair)]
        xmine = jnp.broadcast_to(jnp.concatenate(xmine, axis=0), (NX, NC * NY * CJ, F * H * W))
        got = lax.all_to_all(jnp.concatenate([terms, xmine], axis=1), "x", 0, 0, tiled=True)
    with jax.named_scope("weight_part"):
        local, outer = pl.pallas_call(
            weight_kernel,
            out_shape=[
                jax.ShapeDtypeStruct((NZ, CHUNK + W, CO), jnp.float32),
                jax.ShapeDtypeStruct((F * NX * CJ, NC * NY * W), jnp.bfloat16),
            ],
            in_specs=[smem] + [vmem] * 3,
            out_specs=[vmem] * 2,
            scratch_shapes=[pltpu.VMEM((10, NX * CJ, CO), jnp.float32)],
            compiler_params=params,
        )(jnp.stack([core, row]), strip, pair, got)
    with jax.named_scope("weight_edge"):
        local = pl.pallas_call(
            edge_kernel,
            out_shape=jax.ShapeDtypeStruct(local.shape, jnp.float32),
            in_specs=[vmem] * 3,
            out_specs=vmem,
            input_output_aliases={2: 0},
            compiler_params=params,
        )(outer, edge, local)
    with jax.named_scope("weight_sum"):
        shares = lax.all_to_all(local, "z", 0, 0, tiled=True)
        scale = 1.0 / math.sqrt(NZ * NY * NC * F * H * W)
        mine = (jnp.sum(shares[:, :CHUNK], axis=0) * scale).astype(jnp.bfloat16)
    with jax.named_scope("gather_far"):
        far = lax.all_to_all(
            jnp.broadcast_to(mine, (16, CHUNK, CO)), TILE, 0, 0, axis_index_groups=SPARSE, tiled=True
        )
    with jax.named_scope("gather_near"):
        near = lax.all_to_all(
            jnp.broadcast_to(far, (4, 16, CHUNK, CO)), TILE, 0, 0, axis_index_groups=BLOCKS, tiled=True
        )
    with jax.named_scope("order"):
        near = near.reshape(2, 2, 2, 2, 4, 7, CJ, CO)
        half = jnp.transpose(near, (2, 5, 3, 0, 4, 1, 6, 7)).reshape(14, CIN, CO)
    with jax.named_scope("swap"):
        other = lax.ppermute(half, "core", swap)
        first = jnp.where(core == 0, half, other)
        second = jnp.where(core == 0, other, half)
        order = [
            (first[0:3], first[9:12], second[0:3]),
            (first[3:6], first[12:14], second[9:10], second[3:6]),
            (first[6:9], second[10:13], second[6:9]),
        ]
        full = jnp.concatenate([piece for row_taps in order for piece in row_taps], axis=0)
        weight_grad = full.reshape(3, 3, 3, CIN, CO)
    with jax.named_scope("input_sum"):
        source = lax.broadcasted_iota(jnp.int32, (NZ, W, F * CI), 0)
        edges = shares[:, CHUNK:]
        above = jnp.sum(jnp.where(source < row, edges, 0.0), axis=0)
        below = jnp.sum(jnp.where(source > row, edges, 0.0), axis=0)
        inner = got[:, W : EXT - W].astype(jnp.float32) + got[:, EXT + W : TERMS - W].astype(jnp.float32)
        total = jnp.sum(inner, axis=0).reshape(H, W, F * CI)
        total = jnp.concatenate([total[:1] + above, total[1:-1], total[-1:] + below], axis=0)
        total = total.astype(jnp.bfloat16).reshape(H, W, F, CI)
        input_grad = jnp.transpose(total, (2, 0, 1, 3))[None]
    return (input_grad, weight_grad)


def solution(mesh):
    grid = Mesh(mesh.devices.reshape(NZ, NY, NC, NX), AXES)
    in_specs = (
        P(TILE, None, None, None, "x"),
        P(TILE, None, None, None, "x"),
        P(None, None, None, None, "x"),
    )
    out_specs = (P(TILE, None, None, None, "x"), P(None, None, None, None, "x"))
    return jax.shard_map(shards, mesh=grid, in_specs=in_specs, out_specs=out_specs, check_vma=False)
```
